32 devices in a mesh: seq: 8 (over y, x, core), tp: 4 (over z).
Axes of the slice: x: 2, y: 2, z: 4, core: 2. Of those that a mesh axis runs over, the one named last changes fastest.
Arguments:
- hidden_states: bfloat16 [12288, 8192], P('seq', 'tp'), may hold values from -72 to 72
- positions: int32 [12288], P(('seq', 'tp')), may hold values from 0 to 32767
- key_weight: bfloat16 [8192, 1024], P('tp'), may hold values from -0.0625 to 0.0625
- value_weight: bfloat16 [8192, 1024], P('tp'), may hold values from -0.0625 to 0.0625
Outputs:
- keys: bfloat16 [12288, 1024], P(('seq', 'tp'))
- values: bfloat16 [12288, 1024], P(('seq', 'tp'))
- codes: bfloat16 [12288, 1024], P(('seq', 'tp'))
- page_bounds: float32 [1024, 2, 96], P(('seq', 'tp'))
The draws below stay inside these ranges and needn't reach their ends.
All inputs are finite; a program needn't handle non-finite values.
Results may differ from the reference program's by a relative error of at most 0.008.
Values may be sent and summed in bfloat16 or wider, within the bound.
A program may use at most 128 MiB of HBM per device.

```python
import jax
import jax.numpy as jnp
from jax import lax

D = 8192
KV_HEADS = 8
HEAD = 128
PAGE = 128
TOK_DEV = 1536
KVC = 1024
TOKENS = 12288
PAGES = 96
N_SEQ = 8


def draw_hidden_states(key, part):
    key = jax.random.fold_in(key, 11)
    normal_part = jnp.clip(jax.random.normal(key, (TOKENS, D), jnp.float32), -6.0, 6.0)
    ramp = jnp.arange(TOKENS).astype(jnp.float32) / (TOKENS - 1)
    row_scale = 1.0 + 2.0 * ramp
    return (normal_part * row_scale[:, None]).astype(jnp.bfloat16)


def plant(drawn, stream_key, low, largest):
    extent = drawn.shape
    place = [jax.random.randint(jax.random.fold_in(stream_key, axis), (), 0, extent[axis]) for axis in range(len(extent))]
    drawn = drawn.at[tuple(place)].set(low)
    longest = extent.index(max(extent))
    place[longest] = (place[longest] + 1) % extent[longest]
    return drawn.at[tuple(place)].set(largest)


def block_scale(stream_key, dims, shards, smallest, high):
    factor_of = 1.0
    for dim, shards_of in shards:
        steps = jax.random.uniform(jax.random.fold_in(jax.random.fold_in(stream_key, 6), dim), (shards_of,), jnp.float32, smallest / len(shards), high / len(shards))
        factor_of = factor_of * jnp.repeat(jnp.exp(steps), dims[dim] // shards_of).reshape((-1,) + (1,) * (len(dims) - 1 - dim))
    return factor_of


def centred(stream_key, extent, spread, reach, pieces=(), dtype=jnp.bfloat16):
    factor_of = block_scale(stream_key, extent, pieces, -0.22, 0.18) if pieces else 1.0
    values = jax.random.normal(stream_key, extent, jnp.float32) * spread * factor_of
    return jnp.minimum(jnp.maximum(values, -reach), reach).astype(dtype)


def setup_inputs(seed: int = 0) -> dict:
    key_of = jax.random.split(jax.random.key(seed), 5)
    return {
        "hidden_states": draw_hidden_states(jax.random.fold_in(key_of[4], 71), 0),
        "positions": plant(jax.random.randint(key_of[1], (TOKENS,), 0, 32768), jax.random.fold_in(key_of[1], 1), 0, 32767).astype(jnp.int32),
        "key_weight": centred(key_of[2], (D, KVC), D ** -0.5, 0.0625, ((0, 4),)),
        "value_weight": centred(key_of[3], (D, KVC), D ** -0.5, 0.0625, ((0, 4),)),
    }


def rotate_keys(field, positions):
    count = field.shape[0]
    heads = field.reshape(count, KV_HEADS, HEAD)
    half_width = HEAD // 2
    index = jnp.arange(half_width).astype(jnp.float32)
    frequency = jnp.exp(-jnp.log(jnp.float32(500000.0)) * 2.0 * index / HEAD)
    angles = positions.astype(jnp.float32)[:, None] * frequency[None, :]
    cosine = jnp.cos(angles)[:, None, :]
    sine = jnp.sin(angles)[:, None, :]
    front_half = heads[..., :half_width]
    back_half = heads[..., half_width:]
    turned = jnp.concatenate([front_half * cosine - back_half * sine, back_half * cosine + front_half * sine], axis=-1)
    return turned.reshape(count, KV_HEADS * HEAD)


def reference(hidden_states, positions, key_weight, value_weight):
    blocks = hidden_states.reshape(N_SEQ, TOK_DEV, D)

    def project(block):
        return (jnp.dot(block, key_weight, preferred_element_type=jnp.float32),
                jnp.dot(block, value_weight, preferred_element_type=jnp.float32))

    raw_keys, raw_values = lax.map(project, blocks)
    raw_keys = raw_keys.reshape(TOKENS, KVC)
    values = raw_values.reshape(TOKENS, KVC).astype(jnp.bfloat16)
    peak = jnp.max(jnp.abs(raw_keys), axis=0)
    scale = (peak + 1e-6) / 7.0
    ratio = raw_keys / scale
    codes = (ratio - jnp.sin(2.0 * jnp.pi * ratio) / (2.0 * jnp.pi)).astype(jnp.bfloat16)
    dequant = codes.astype(jnp.float32) * scale
    rotated = rotate_keys(dequant, positions)
    keys = rotated.astype(jnp.bfloat16)
    paged = rotated.reshape(PAGES, PAGE, KVC)
    page_low = jnp.min(paged, axis=1)
    page_high = jnp.max(paged, axis=1)
    page_bounds = jnp.transpose(jnp.stack([page_low, page_high], axis=0), (2, 0, 1))
    return keys, values, codes, page_bounds
```

```python
import functools
import math

import jax
import jax.numpy as jnp
from jax import lax
from jax.experimental import pallas as pl
from jax.experimental.pallas import tpu as pltpu
from jax.sharding import PartitionSpec as P

HEAD = 128
PAGE = 128
CW = 256
DEPTH = 4
MESH = pl.DeviceIdType.MESH


def sine_of_turns(turns):
    rest = turns - jnp.round(turns)
    size = jnp.abs(rest)
    x = (2.0 * math.pi) * jnp.minimum(size, 0.5 - size)
    y = x * x
    poly = jnp.float32(-1.0 / math.factorial(11))
    for order, sign in ((9, 1.0), (7, -1.0), (5, 1.0), (3, -1.0), (1, 1.0)):
        poly = poly * y + jnp.float32(sign / math.factorial(order))
    wave = poly * x
    return jnp.where(rest < 0.0, -wave, wave)


def kernel(
    n_seq, n_tp,
    hidden, pos, key_w, value_w,
    keys_out, values_out, codes_out, bounds_out,
    hb, wb, sb, rr, rl, acc, raw, cos_s, sin_s,
    keys_s, codes_s, values_s,
    peak_own, peak_tp, peak_mid, peak_seq,
    bnd_own, bnd_seq, bnd_tp, bnd_pages, bnd_turned, bnd_res,
    h_sem, w_sem, send_sem, rr_sem, rl_sem, out_sem,
    ptp_send, ptp_recv, psq_send, psq_recv, bsq_send, bsq_recv, btp_send, btp_recv,
):
    s = lax.axis_index("seq")
    t = lax.axis_index("tp")
    rows = hb.shape[1]
    width = raw.shape[1]
    nch = width // CW
    per_phase = (n_tp - 1) * nch
    steps = 2 * per_phase
    pages = rows // PAGE

    def load_h(b):
        return pltpu.make_async_copy(hidden.at[pl.ds(b * rows, rows), :], hb.at[b], h_sem.at[b])

    def load_w(ch):
        src = key_w if ch < nch else value_w
        return pltpu.make_async_copy(src.at[:, pl.ds((ch % nch) * CW, CW)], wb.at[ch], w_sem.at[ch])

    load_w(0).start()
    load_h(n_tp - 1).start()
    load_h(0).start()
    for ch in range(1, nch):
        load_w(ch).start()
    for b in range(1, n_tp - 1):
        load_h(b).start()
    for ch in range(nch, 2 * nch):
        load_w(ch).start()

    barrier = pltpu.get_barrier_semaphore()
    for d in range(1, n_tp):
        pl.semaphore_signal(barrier, inc=1, device_id={"tp": lax.rem(t + d, n_tp)}, device_id_type=MESH)
    for d in range(1, n_seq):
        pl.semaphore_signal(barrier, inc=1, device_id={"seq": lax.rem(s + d, n_seq)}, device_id_type=MESH)
    pl.semaphore_wait(barrier, n_tp - 1 + n_seq - 1)

    def send_right(b, ch):
        return pltpu.make_async_remote_copy(
            sb.at[b, ch], rr.at[b, ch], send_sem.at[b, ch], rr_sem.at[b, ch],
            device_id={"tp": jnp.minimum(t + 1, n_tp - 1)}, device_id_type=MESH)

    def send_left(b, ch):
        return pltpu.make_async_remote_copy(
            sb.at[b, ch], rl.at[b, ch], send_sem.at[b, ch], rl_sem.at[b, ch],
            device_id={"tp": jnp.maximum(t - 1, 0)}, device_id_type=MESH)

    def place(i):
        q = lax.rem(i, per_phase)
        turn = q // nch
        c = lax.rem(q, nch)
        return turn, c, (i // per_phase) * nch + c

    def wait_sends(i):
        turn, _, ch = place(i)

        @pl.when(n_tp - 1 - turn > t)
        def _():
            send_right(n_tp - 1 - turn, ch).wait_send()

        @pl.when(turn < t)
        def _():
            send_left(turn, ch).wait_send()

    def fill_angles():
        lane = lax.broadcasted_iota(jnp.int32, (1, HEAD), 1)
        half = HEAD // 2
        index = jnp.where(lane < half, lane, lane - half).astype(jnp.float32)
        frequency = jnp.exp(-jnp.log(jnp.float32(500000.0)) * 2.0 * index / HEAD)
        for j in range(pages):
            row = pos[j:j + 1, :].astype(jnp.float32)
            column = jnp.transpose(jnp.broadcast_to(row, (PAGE, PAGE)))
            angles = column * frequency
            sine = jnp.sin(angles)
            cos_s[j * PAGE:(j + 1) * PAGE, :] = jnp.cos(angles)
            sin_s[j * PAGE:(j + 1) * PAGE, :] = jnp.where(lane < half, -sine, sine)

    def own_sum(ch):
        acc[...] = jnp.dot(hb[t], wb[ch], preferred_element_type=jnp.float32)

        @pl.when(t > 0)
        def _():
            send_right(t, ch).wait_recv()
            acc[...] += rr[t, ch].astype(jnp.float32)

        @pl.when(t < n_tp - 1)
        def _():
            send_left(t, ch).wait_recv()
            acc[...] += rl[t, ch].astype(jnp.float32)

    def tp_copies(src, dst, send, recv, own):
        return [
            pltpu.make_async_remote_copy(
                src, dst.at[t if own else d], send.at[d], recv.at[d],
                device_id={"tp": lax.rem(t + d, n_tp)}, device_id_type=MESH)
            for d in range(1, n_tp)
        ]

    def peak_tp_copies():
        return tp_copies(peak_own, peak_tp, ptp_send, ptp_recv, False)

    def peak_seq_copies():
        return [
            pltpu.make_async_remote_copy(
                peak_mid, peak_seq.at[d], psq_send.at[d], psq_recv.at[d],
                device_id={"seq": lax.rem(s + d, n_seq)}, device_id_type=MESH)
            for d in range(1, n_seq)
        ]

    group = width // n_seq
    tile = bnd_seq.shape[2]

    def tile_of(other):
        return pl.ds(pl.multiple_of((other * group) // tile * tile, 128), tile)

    def bound_seq_copies():
        out = []
        for d in range(1, n_seq):
            other = lax.rem(s + d, n_seq)
            out.append(pltpu.make_async_remote_copy(
                bnd_own.at[:, tile_of(other)], bnd_seq.at[s], bsq_send.at[d], bsq_recv.at[d],
                device_id={"seq": other}, device_id_type=MESH))
        return out

    def bound_tp_copies():
        return tp_copies(bnd_seq, bnd_tp, btp_send, btp_recv, True)

    def key_sums():
        def one(c, carry):
            own_sum(c)
            total = acc[...]
            lanes = pl.ds(pl.multiple_of(c * CW, 128), CW)
            raw[:, lanes] = total
            peak_own[:, lanes] = jnp.max(jnp.abs(total).reshape(rows // 8, 8, CW), axis=0)
            return carry

        lax.fori_loop(0, nch, one, 0)
        for copy in peak_tp_copies():
            copy.start()

    def peak_middle():
        best = peak_own[...]
        for copy in peak_tp_copies():
            copy.wait_recv()
        for d in range(1, n_tp):
            best = jnp.maximum(best, peak_tp[d])
        peak_mid[...] = best
        for copy in peak_seq_copies():
            copy.start()

    def finish_keys():
        for copy in peak_seq_copies():
            copy.wait_recv()
        best = peak_mid[...]
        for d in range(1, n_seq):
            best = jnp.maximum(best, peak_seq[d])
        peak_tp[0] = best
        bnd_own[...] = jnp.zeros_like(bnd_own)

        def one(h, carry):
            lanes = pl.ds(pl.multiple_of(h * HEAD, 128), HEAD)
            peak = jnp.max(peak_tp[0, :, lanes], axis=0, keepdims=True)
            scale = (peak + 1e-06) / 7.0
            inverse = 1.0 / scale
            for j in range(pages):
                part = pl.ds(j * PAGE, PAGE)
                ratio = raw[part, lanes] * inverse
                code = (ratio - sine_of_turns(ratio) * (1.0 / (2.0 * math.pi))).astype(jnp.bfloat16)
                codes_s[part, lanes] = code
                dequant = code.astype(jnp.float32) * scale
                turned = dequant * cos_s[part, :] + pltpu.roll(dequant, HEAD // 2, 1) * sin_s[part, :]
                keys_s[part, lanes] = turned.astype(jnp.bfloat16)
                bnd_own[j:j + 1, lanes] = jnp.min(turned, axis=0, keepdims=True)
                bnd_own[pages + j:pages + j + 1, lanes] = jnp.max(turned, axis=0, keepdims=True)
            return carry

        lax.fori_loop(0, width // HEAD, one, 0)
        for copy in bound_seq_copies():
            copy.start()
        pltpu.make_async_copy(codes_s, codes_out, out_sem.at[0]).start()
        pltpu.make_async_copy(keys_s, keys_out, out_sem.at[1]).start()
        bnd_seq[s] = bnd_own[:, tile_of(s)]

    def bounds_middle():
        for copy in bound_seq_copies():
            copy.wait_recv()
        for copy in bound_tp_copies():
            copy.start()
        bnd_tp[t] = bnd_seq[...]

    def finish_bounds():
        for copy in bound_tp_copies():
            copy.wait_recv()
        channels = width // (n_seq * n_tp)
        inside = lax.rem(s * group, tile) + t * channels
        for side in range(2):
            bnd_pages[...] = jnp.zeros_like(bnd_pages)
            for a in range(n_seq):
                for b in range(n_tp):
                    first = (a * n_tp + b) * pages
                    bnd_pages[first:first + pages, :] = bnd_tp[b, a, side * pages:(side + 1) * pages, :]
            bnd_turned[...] = jnp.transpose(bnd_pages[...])
            mine = bnd_turned[pl.ds(pl.multiple_of(inside, 8), channels), :]
            bnd_res[side] = mine[:, :bnd_res.shape[2]]
        pltpu.make_async_copy(bnd_res, bounds_out, out_sem.at[2]).start()

    def body(i, carry):
        turn, c, ch = place(i)

        @pl.when(turn == 0)
        def _():
            pltpu.make_async_copy(key_w.at[:, pl.ds(0, CW)], wb.at[ch], w_sem.at[ch]).wait()

        for o in range(n_tp // 2):
            @pl.when(i == o * nch)
            def _(o=o):
                load_h(o).wait()
                load_h(n_tp - 1 - o).wait()

        @pl.when(i >= DEPTH)
        def _():
            wait_sends(i - DEPTH)

        right = n_tp - 1 - turn
        left = turn

        @pl.when(right > t)
        def _():
            acc[...] = jnp.dot(hb[right], wb[ch], preferred_element_type=jnp.float32)

            @pl.when(t > 0)
            def _():
                send_right(right, ch).wait_recv()
                acc[...] += rr[right, ch].astype(jnp.float32)

            sb[right, ch] = acc[...].astype(jnp.bfloat16)
            send_right(right, ch).start()

        @pl.when(left < t)
        def _():
            acc[...] = jnp.dot(hb[left], wb[ch], preferred_element_type=jnp.float32)

            @pl.when(t < n_tp - 1)
            def _():
                send_left(left, ch).wait_recv()
                acc[...] += rl[left, ch].astype(jnp.float32)

            sb[left, ch] = acc[...].astype(jnp.bfloat16)
            send_left(left, ch).start()

        for when, work in (
            (2, fill_angles),
            (per_phase, key_sums),
            (per_phase + 1, peak_middle),
            (per_phase + 3, finish_keys),
            (per_phase + 5, bounds_middle),
            (per_phase + 7, finish_bounds),
        ):
            pl.when(i == when)(work)
        return carry

    lax.fori_loop(0, steps, body, 0)

    def last(c, carry):
        own_sum(nch + c)
        values_s[c] = acc[...].astype(jnp.bfloat16)
        lanes = pl.ds(pl.multiple_of(c * CW, 128), CW)
        pltpu.make_async_copy(values_s.at[c], values_out.at[:, lanes], out_sem.at[3 + c]).start()
        return carry

    lax.fori_loop(0, nch, last, 0)

    def drain(i, carry):
        wait_sends(i)
        return carry

    lax.fori_loop(steps - DEPTH, steps, drain, 0)
    for copy in peak_tp_copies() + peak_seq_copies() + bound_seq_copies() + bound_tp_copies():
        copy.wait_send()
    pltpu.make_async_copy(codes_s, codes_out, out_sem.at[0]).wait()
    pltpu.make_async_copy(keys_s, keys_out, out_sem.at[1]).wait()
    pltpu.make_async_copy(bnd_res, bounds_out, out_sem.at[2]).wait()
    for c in range(nch):
        pltpu.make_async_copy(values_s.at[c], values_out.at[:, pl.ds(c * CW, CW)], out_sem.at[3 + c]).wait()


def per_device(n_seq, n_tp, hidden_states, positions, key_weight, value_weight):
    depth, width = key_weight.shape
    rows = hidden_states.shape[0] // n_tp
    nch = width // CW
    pages = rows // PAGE
    all_pages = pages * n_seq * n_tp
    padded_pages = -(-all_pages // 128) * 128
    tile = max(128, width // n_seq)
    channels = width // (n_seq * n_tp)
    bf16, f32 = jnp.bfloat16, jnp.float32
    dma = pltpu.SemaphoreType.DMA
    hbm = pl.BlockSpec(memory_space=pl.ANY)
    keys, values, codes, bounds = pl.pallas_call(
        functools.partial(kernel, n_seq, n_tp),
        out_shape=(
            jax.ShapeDtypeStruct((rows, width), bf16),
            jax.ShapeDtypeStruct((rows, width), bf16),
            jax.ShapeDtypeStruct((rows, width), bf16),
            jax.ShapeDtypeStruct((2, channels, all_pages), f32),
        ),
        in_specs=[hbm, pl.BlockSpec(memory_space=pltpu.VMEM), hbm, hbm],
        out_specs=(hbm, hbm, hbm, hbm),
        scratch_shapes=[
            pltpu.VMEM((n_tp, rows, depth), bf16),
            pltpu.VMEM((2 * nch, depth, CW), bf16),
            pltpu.VMEM((n_tp, 2 * nch, rows, CW), bf16),
            pltpu.VMEM((n_tp, 2 * nch, rows, CW), bf16),
            pltpu.VMEM((n_tp, 2 * nch, rows, CW), bf16),
            pltpu.VMEM((rows, CW), f32),
            pltpu.VMEM((rows, width), f32),
            pltpu.VMEM((rows, HEAD), f32),
            pltpu.VMEM((rows, HEAD), f32),
            pltpu.VMEM((rows, width), bf16),
            pltpu.VMEM((rows, width), bf16),
            pltpu.VMEM((nch, rows, CW), bf16),
            pltpu.VMEM((8, width), f32),
            pltpu.VMEM((n_tp, 8, width), f32),
            pltpu.VMEM((8, width), f32),
            pltpu.VMEM((n_seq, 8, width), f32),
            pltpu.VMEM((8, width), f32),
            pltpu.VMEM((n_seq, 8, tile), f32),
            pltpu.VMEM((n_tp, n_seq, 8, tile), f32),
            pltpu.VMEM((padded_pages, tile), f32),
            pltpu.VMEM((tile, padded_pages), f32),
            pltpu.VMEM((2, channels, all_pages), f32),
            dma((n_tp,)),
            dma((2 * nch,)),
            dma((n_tp, 2 * nch)),
            dma((n_tp, 2 * nch)),
            dma((n_tp, 2 * nch)),
            dma((3 + nch,)),
            dma((n_tp,)), dma((n_tp,)),
            dma((n_seq,)), dma((n_seq,)),
            dma((n_seq,)), dma((n_seq,)),
            dma((n_tp,)), dma((n_tp,)),
        ],
        compiler_params=pltpu.CompilerParams(
            collective_id=0, has_side_effects=True, vmem_limit_bytes=56 * 2**20
        ),
        cost_estimate=pl.CostEstimate(
            flops=2 * n_tp * rows * depth * 2 * width,
            bytes_accessed=2 * (n_tp * rows * depth + 2 * depth * width + 3 * rows * width),
            transcendentals=0,
        ),
    )(hidden_states, positions.reshape(pages, PAGE), key_weight, value_weight)
    return keys, values, codes, jnp.transpose(bounds, (1, 0, 2))


def solution(mesh):
    return jax.shard_map(
        functools.partial(per_device, mesh.shape["seq"], mesh.shape["tp"]),
        mesh=mesh,
        in_specs=(P("seq", "tp"), P(("seq", "tp")), P("tp", None), P("tp", None)),
        out_specs=(
            P(("seq", "tp"), None),
            P(("seq", "tp"), None),
            P(("seq", "tp"), None),
            P(("seq", "tp"), None, None),
        ),
        check_vma=False,
    )
```

```python
import functools
import math

import jax
import jax.numpy as jnp
from jax import lax
from jax.experimental import pallas as pl
from jax.experimental.pallas import tpu as pltpu
from jax.sharding import PartitionSpec as P

HEAD = 128
PAGE = 128
CW = 256
DEPTH = 12
MESH = pl.DeviceIdType.MESH


def sine_of_turns(turns):
    rest = turns - jnp.round(turns)
    size = jnp.abs(rest)
    x = (2.0 * math.pi) * jnp.minimum(size, 0.5 - size)
    y = x * x
    poly = jnp.float32(-1.0 / math.factorial(11))
    for order, sign in ((9, 1.0), (7, -1.0), (5, 1.0), (3, -1.0), (1, 1.0)):
        poly = poly * y + jnp.float32(sign / math.factorial(order))
    wave = poly * x
    return jnp.where(rest < 0.0, -wave, wave)


def kernel(
    n_seq, n_tp,
    hidden, pos, key_w, value_w,
    keys_out, values_out, codes_out, bounds_out,
    hb, wb, sb, rr, rl, acc, raw, cos_s, sin_s,
    keys_s, codes_s, values_s,
    peak_own, peak_tp, peak_mid, peak_seq,
    bnd_own, bnd_seq, bnd_tp, bnd_pages, bnd_turned, bnd_res,
    h_sem, w_sem, send_sem, rr_sem, rl_sem, out_sem,
    ptp_send, ptp_recv, psq_send, psq_recv, bsq_send, bsq_recv, btp_send, btp_recv,
):
    s = lax.axis_index("seq")
    t = lax.axis_index("tp")
    rows = hb.shape[1]
    width = raw.shape[1]
    nch = width // CW
    per_phase = (n_tp - 1) * nch
    steps = 2 * per_phase
    pages = rows // PAGE

    def load_h(b):
        return pltpu.make_async_copy(hidden.at[pl.ds(b * rows, rows), :], hb.at[b], h_sem.at[b])

    def load_w(ch):
        src = key_w if ch < nch else value_w
        return pltpu.make_async_copy(src.at[:, pl.ds((ch % nch) * CW, CW)], wb.at[ch], w_sem.at[ch])

    load_w(0).start()
    load_h(n_tp - 1).start()
    load_h(0).start()
    for ch in range(1, nch):
        load_w(ch).start()
    for b in range(1, n_tp - 1):
        load_h(b).start()
    for ch in range(nch, 2 * nch):
        load_w(ch).start()

    barrier = pltpu.get_barrier_semaphore()
    for d in range(1, n_tp):
        pl.semaphore_signal(barrier, inc=1, device_id={"tp": lax.rem(t + d, n_tp)}, device_id_type=MESH)
    for d in range(1, n_seq):
        pl.semaphore_signal(barrier, inc=1, device_id={"seq": lax.rem(s + d, n_seq)}, device_id_type=MESH)
    pl.semaphore_wait(barrier, n_tp - 1 + n_seq - 1)

    def send_right(b, ch):
        return pltpu.make_async_remote_copy(
            sb.at[b, ch], rr.at[b, ch], send_sem.at[b, ch], rr_sem.at[b, ch],
            device_id={"tp": jnp.minimum(t + 1, n_tp - 1)}, device_id_type=MESH)

    def send_left(b, ch):
        return pltpu.make_async_remote_copy(
            sb.at[b, ch], rl.at[b, ch], send_sem.at[b, ch], rl_sem.at[b, ch],
            device_id={"tp": jnp.maximum(t - 1, 0)}, device_id_type=MESH)

    def place(i):
        q = lax.rem(i, per_phase)
        turn = q // nch
        c = lax.rem(q, nch)
        return turn, c, (i // per_phase) * nch + c

    def right_job(j, run):
        turn, _, ch = place(jnp.clip(j, 0, steps - 1))
        b = n_tp - 1 - turn

        @pl.when((j >= 0) & (j < steps) & (b > t))
        def _():
            run(b, ch)

    def left_job(j, run):
        turn, _, ch = place(jnp.clip(j, 0, steps - 1))

        @pl.when((j >= 0) & (j < steps) & (turn < t))
        def _():
            run(turn, ch)

    def wait_sends(i):
        right_job(i - t, lambda b, ch: send_right(b, ch).wait_send())
        left_job(i - (n_tp - 1 - t), lambda b, ch: send_left(b, ch).wait_send())

    def fill_angles():
        lane = lax.broadcasted_iota(jnp.int32, (1, HEAD), 1)
        half = HEAD // 2
        index = jnp.where(lane < half, lane, lane - half).astype(jnp.float32)
        frequency = jnp.exp(-jnp.log(jnp.float32(500000.0)) * 2.0 * index / HEAD)
        for j in range(pages):
            row = pos[j:j + 1, :].astype(jnp.float32)
            column = jnp.transpose(jnp.broadcast_to(row, (PAGE, PAGE)))
            angles = column * frequency
            sine = jnp.sin(angles)
            cos_s[j * PAGE:(j + 1) * PAGE, :] = jnp.cos(angles)
            sin_s[j * PAGE:(j + 1) * PAGE, :] = jnp.where(lane < half, -sine, sine)

    def own_sum(ch):
        acc[...] = jnp.dot(hb[t], wb[ch], preferred_element_type=jnp.float32)

        @pl.when(t > 0)
        def _():
            send_right(t, ch).wait_recv()
            acc[...] += rr[t, ch].astype(jnp.float32)

        @pl.when(t < n_tp - 1)
        def _():
            send_left(t, ch).wait_recv()
            acc[...] += rl[t, ch].astype(jnp.float32)

    def tp_copies(src, dst, send, recv, own):
        return [
            pltpu.make_async_remote_copy(
                src, dst.at[t if own else d], send.at[d], recv.at[d],
                device_id={"tp": lax.rem(t + d, n_tp)}, device_id_type=MESH)
            for d in range(1, n_tp)
        ]

    def peak_tp_copies():
        return tp_copies(peak_own, peak_tp, ptp_send, ptp_recv, False)

    def peak_seq_copies():
        return [
            pltpu.make_async_remote_copy(
                peak_mid, peak_seq.at[d], psq_send.at[d], psq_recv.at[d],
                device_id={"seq": lax.rem(s + d, n_seq)}, device_id_type=MESH)
            for d in range(1, n_seq)
        ]

    group = width // n_seq
    tile = bnd_seq.shape[2]

    def tile_of(other):
        return pl.ds(pl.multiple_of((other * group) // tile * tile, 128), tile)

    def bound_seq_copies():
        out = []
        for d in range(1, n_seq):
            other = lax.rem(s + d, n_seq)
            out.append(pltpu.make_async_remote_copy(
                bnd_own.at[:, tile_of(other)], bnd_seq.at[s], bsq_send.at[d], bsq_recv.at[d],
                device_id={"seq": other}, device_id_type=MESH))
        return out

    def bound_tp_copies():
        return tp_copies(bnd_seq, bnd_tp, btp_send, btp_recv, True)

    def key_sums():
        def one(c, carry):
            own_sum(c)
            total = acc[...]
            lanes = pl.ds(pl.multiple_of(c * CW, 128), CW)
            raw[:, lanes] = total
            peak_own[:, lanes] = jnp.max(jnp.abs(total).reshape(rows // 8, 8, CW), axis=0)
            return carry

        lax.fori_loop(0, nch, one, 0)
        for copy in peak_tp_copies():
            copy.start()

    def peak_middle():
        best = peak_own[...]
        for copy in peak_tp_copies():
            copy.wait_recv()
        for d in range(1, n_tp):
            best = jnp.maximum(best, peak_tp[d])
        peak_mid[...] = best
        for copy in peak_seq_copies():
            copy.start()

    def finish_keys():
        for copy in peak_seq_copies():
            copy.wait_recv()
        best = peak_mid[...]
        for d in range(1, n_seq):
            best = jnp.maximum(best, peak_seq[d])
        peak_tp[0] = best
        bnd_own[...] = jnp.zeros_like(bnd_own)

        def one(h, carry):
            lanes = pl.ds(pl.multiple_of(h * HEAD, 128), HEAD)
            peak = jnp.max(peak_tp[0, :, lanes], axis=0, keepdims=True)
            scale = (peak + 1e-06) / 7.0
            inverse = 1.0 / scale
            for j in range(pages):
                part = pl.ds(j * PAGE, PAGE)
                ratio = raw[part, lanes] * inverse
                code = (ratio - sine_of_turns(ratio) * (1.0 / (2.0 * math.pi))).astype(jnp.bfloat16)
                codes_s[part, lanes] = code
                dequant = code.astype(jnp.float32) * scale
                turned = dequant * cos_s[part, :] + pltpu.roll(dequant, HEAD // 2, 1) * sin_s[part, :]
                keys_s[part, lanes] = turned.astype(jnp.bfloat16)
                bnd_own[j:j + 1, lanes] = jnp.min(turned, axis=0, keepdims=True)
                bnd_own[pages + j:pages + j + 1, lanes] = jnp.max(turned, axis=0, keepdims=True)
            return carry

        lax.fori_loop(0, width // HEAD, one, 0)
        for copy in bound_seq_copies():
            copy.start()
        pltpu.make_async_copy(codes_s, codes_out, out_sem.at[0]).start()
        pltpu.make_async_copy(keys_s, keys_out, out_sem.at[1]).start()
        bnd_seq[s] = bnd_own[:, tile_of(s)]

    def bounds_middle():
        for copy in bound_seq_copies():
            copy.wait_recv()
        for copy in bound_tp_copies():
            copy.start()
        bnd_tp[t] = bnd_seq[...]

    def finish_bounds():
        for copy in bound_tp_copies():
            copy.wait_recv()
        channels = width // (n_seq * n_tp)
        inside = lax.rem(s * group, tile) + t * channels
        for side in range(2):
            bnd_pages[...] = jnp.zeros_like(bnd_pages)
            for a in range(n_seq):
                for b in range(n_tp):
                    first = (a * n_tp + b) * pages
                    bnd_pages[first:first + pages, :] = bnd_tp[b, a, side * pages:(side + 1) * pages, :]
            bnd_turned[...] = jnp.transpose(bnd_pages[...])
            mine = bnd_turned[pl.ds(pl.multiple_of(inside, 8), channels), :]
            bnd_res[side] = mine[:, :bnd_res.shape[2]]
        pltpu.make_async_copy(bnd_res, bounds_out, out_sem.at[2]).start()

    def forward_right(b, ch):
        acc[...] = jnp.dot(hb[b], wb[ch], preferred_element_type=jnp.float32)

        @pl.when(t > 0)
        def _():
            send_right(b, ch).wait_recv()
            acc[...] += rr[b, ch].astype(jnp.float32)

        sb[b, ch] = acc[...].astype(jnp.bfloat16)
        send_right(b, ch).start()

    def forward_left(b, ch):
        acc[...] = jnp.dot(hb[b], wb[ch], preferred_element_type=jnp.float32)

        @pl.when(t < n_tp - 1)
        def _():
            send_left(b, ch).wait_recv()
            acc[...] += rl[b, ch].astype(jnp.float32)

        sb[b, ch] = acc[...].astype(jnp.bfloat16)
        send_left(b, ch).start()

    def body(i, carry):
        turn, c, ch = place(jnp.minimum(i, steps - 1))

        @pl.when((turn == 0) & (i < steps))
        def _():
            pltpu.make_async_copy(key_w.at[:, pl.ds(0, CW)], wb.at[ch], w_sem.at[ch]).wait()

        for o in range(n_tp // 2):
            @pl.when(i == o * nch)
            def _(o=o):
                load_h(o).wait()
                load_h(n_tp - 1 - o).wait()

        wait_sends(i - DEPTH)
        right_job(i - t, forward_right)
        left_job(i - (n_tp - 1 - t), forward_left)

        for when, work in (
            (2, fill_angles),
            (per_phase, key_sums),
            (per_phase + 2, peak_middle),
            (per_phase + 5, finish_keys),
            (per_phase + 7, bounds_middle),
            (per_phase + 9, finish_bounds),
        ):
            pl.when(i == when)(work)
        return carry

    lax.fori_loop(0, steps + n_tp - 2, body, 0)

    def last(c, carry):
        own_sum(nch + c)
        values_s[c] = acc[...].astype(jnp.bfloat16)
        lanes = pl.ds(pl.multiple_of(c * CW, 128), CW)
        pltpu.make_async_copy(values_s.at[c], values_out.at[:, lanes], out_sem.at[3 + c]).start()
        return carry

    lax.fori_loop(0, nch, last, 0)

    def drain(i, carry):
        wait_sends(i)
        return carry

    lax.fori_loop(steps + n_tp - 2 - DEPTH, steps + n_tp - 2, drain, 0)
    for copy in peak_tp_copies() + peak_seq_copies() + bound_seq_copies() + bound_tp_copies():
        copy.wait_send()
    pltpu.make_async_copy(codes_s, codes_out, out_sem.at[0]).wait()
    pltpu.make_async_copy(keys_s, keys_out, out_sem.at[1]).wait()
    pltpu.make_async_copy(bnd_res, bounds_out, out_sem.at[2]).wait()
    for c in range(nch):
        pltpu.make_async_copy(values_s.at[c], values_out.at[:, pl.ds(c * CW, CW)], out_sem.at[3 + c]).wait()


def per_device(n_seq, n_tp, hidden_states, positions, key_weight, value_weight):
    depth, width = key_weight.shape
    rows = hidden_states.shape[0] // n_tp
    nch = width // CW
    pages = rows // PAGE
    all_pages = pages * n_seq * n_tp
    padded_pages = -(-all_pages // 128) * 128
    tile = max(128, width // n_seq)
    channels = width // (n_seq * n_tp)
    bf16, f32 = jnp.bfloat16, jnp.float32
    dma = pltpu.SemaphoreType.DMA
    hbm = pl.BlockSpec(memory_space=pl.ANY)
    keys, values, codes, bounds = pl.pallas_call(
        functools.partial(kernel, n_seq, n_tp),
        out_shape=(
            jax.ShapeDtypeStruct((rows, width), bf16),
            jax.ShapeDtypeStruct((rows, width), bf16),
            jax.ShapeDtypeStruct((rows, width), bf16),
            jax.ShapeDtypeStruct((2, channels, all_pages), f32),
        ),
        in_specs=[hbm, pl.BlockSpec(memory_space=pltpu.VMEM), hbm, hbm],
        out_specs=(hbm, hbm, hbm, hbm),
        scratch_shapes=[
            pltpu.VMEM((n_tp, rows, depth), bf16),
            pltpu.VMEM((2 * nch, depth, CW), bf16),
            pltpu.VMEM((n_tp, 2 * nch, rows, CW), bf16),
            pltpu.VMEM((n_tp, 2 * nch, rows, CW), bf16),
            pltpu.VMEM((n_tp, 2 * nch, rows, CW), bf16),
            pltpu.VMEM((rows, CW), f32),
            pltpu.VMEM((rows, width), f32),
            pltpu.VMEM((rows, HEAD), f32),
            pltpu.VMEM((rows, HEAD), f32),
            pltpu.VMEM((rows, width), bf16),
            pltpu.VMEM((rows, width), bf16),
            pltpu.VMEM((nch, rows, CW), bf16),
            pltpu.VMEM((8, width), f32),
            pltpu.VMEM((n_tp, 8, width), f32),
            pltpu.VMEM((8, width), f32),
            pltpu.VMEM((n_seq, 8, width), f32),
            pltpu.VMEM((8, width), f32),
            pltpu.VMEM((n_seq, 8, tile), f32),
            pltpu.VMEM((n_tp, n_seq, 8, tile), f32),
            pltpu.VMEM((padded_pages, tile), f32),
            pltpu.VMEM((tile, padded_pages), f32),
            pltpu.VMEM((2, channels, all_pages), f32),
            dma((n_tp,)),
            dma((2 * nch,)),
            dma((n_tp, 2 * nch)),
            dma((n_tp, 2 * nch)),
            dma((n_tp, 2 * nch)),
            dma((3 + nch,)),
            dma((n_tp,)), dma((n_tp,)),
            dma((n_seq,)), dma((n_seq,)),
            dma((n_seq,)), dma((n_seq,)),
            dma((n_tp,)), dma((n_tp,)),
        ],
        compiler_params=pltpu.CompilerParams(
            collective_id=0, has_side_effects=True, vmem_limit_bytes=56 * 2**20
        ),
        cost_estimate=pl.CostEstimate(
            flops=2 * n_tp * rows * depth * 2 * width,
            bytes_accessed=2 * (n_tp * rows * depth + 2 * depth * width + 3 * rows * width),
            transcendentals=0,
        ),
    )(hidden_states, positions.reshape(pages, PAGE), key_weight, value_weight)
    return keys, values, codes, jnp.transpose(bounds, (1, 0, 2))


def solution(mesh):
    return jax.shard_map(
        functools.partial(per_device, mesh.shape["seq"], mesh.shape["tp"]),
        mesh=mesh,
        in_specs=(P("seq", "tp"), P(("seq", "tp")), P("tp", None), P("tp", None)),
        out_specs=(
            P(("seq", "tp"), None),
            P(("seq", "tp"), None),
            P(("seq", "tp"), None),
            P(("seq", "tp"), None, None),
        ),
        check_vma=False,
    )
```

```python
import functools
import math

import jax
import jax.numpy as jnp
from jax import lax
from jax.experimental import pallas as pl
from jax.experimental.pallas import tpu as pltpu
from jax.sharding import PartitionSpec as P

HEAD = 128
PAGE = 128
CW = 256
DEPTH = 12
MESH = pl.DeviceIdType.MESH


def sine_of_turns(turns):
    rest = turns - jnp.round(turns)
    size = jnp.abs(rest)
    x = (2.0 * math.pi) * jnp.minimum(size, 0.5 - size)
    y = x * x
    poly = jnp.float32(-1.0 / math.factorial(11))
    for order, sign in ((9, 1.0), (7, -1.0), (5, 1.0), (3, -1.0), (1, 1.0)):
        poly = poly * y + jnp.float32(sign / math.factorial(order))
    wave = poly * x
    return jnp.where(rest < 0.0, -wave, wave)


def kernel(
    n_seq, n_tp,
    hidden, pos, key_w, value_w,
    keys_out, values_out, codes_out, bounds_out,
    hb, wb, sb, rr, rl, acc, raw, cos_s, sin_s,
    keys_s, codes_s, values_s,
    peak_own, peak_tp, peak_mid, peak_seq,
    bnd_own, bnd_seq, bnd_tp, bnd_pages, bnd_turned, bnd_res,
    h_sem, w_sem, send_sem, rr_sem, rl_sem, out_sem,
    ptp_send, ptp_recv, psq_send, psq_recv, bsq_send, bsq_recv, btp_send, btp_recv,
):
    s = lax.axis_index("seq")
    t = lax.axis_index("tp")
    rows = hb.shape[1]
    width = raw.shape[1]
    nch = width // CW
    per_phase = (n_tp - 1) * nch
    steps = 2 * per_phase
    pages = rows // PAGE

    def load_h(b):
        return pltpu.make_async_copy(hidden.at[pl.ds(b * rows, rows), :], hb.at[b], h_sem.at[b])

    def load_w(ch):
        src = key_w if ch < nch else value_w
        return pltpu.make_async_copy(src.at[:, pl.ds((ch % nch) * CW, CW)], wb.at[ch], w_sem.at[ch])

    first = jnp.where(t < n_tp // 2, n_tp - 1, 0)
    second = n_tp - 1 - first
    piece, deep = rows // 3, wb.shape[1] // 2
    for k in range(2):
        part = pl.ds(k * deep, deep)
        pltpu.make_async_copy(key_w.at[part, pl.ds(0, CW)], wb.at[0, part], w_sem.at[0]).start()
    for k in range(3):
        pltpu.make_async_copy(
            hidden.at[pl.ds(first * rows + k * piece, piece), :], hb.at[first, pl.ds(k * piece, piece)], h_sem.at[first]
        ).start()

    barrier = pltpu.get_barrier_semaphore()
    for d in range(1, n_tp):
        pl.semaphore_signal(barrier, inc=1, device_id={"tp": lax.rem(t + d, n_tp)}, device_id_type=MESH)
    for d in range(1, n_seq):
        pl.semaphore_signal(barrier, inc=1, device_id={"seq": lax.rem(s + d, n_seq)}, device_id_type=MESH)

    load_w(0).wait()
    load_h(first).wait()
    for ch in range(1, nch):
        load_w(ch).start()
    load_h(second).start()
    for b in range(1, n_tp - 1):
        load_h(b).start()
    for ch in range(nch, 2 * nch):
        load_w(ch).start()

    @pl.when((t == 0) | (t == n_tp - 1))
    def _():
        sb[first, 0] = jnp.dot(hb[first], wb[0], preferred_element_type=jnp.float32).astype(jnp.bfloat16)

    pl.semaphore_wait(barrier, n_tp - 1 + n_seq - 1)

    def send_right(b, ch):
        return pltpu.make_async_remote_copy(
            sb.at[b, ch], rr.at[b, ch], send_sem.at[b, ch], rr_sem.at[b, ch],
            device_id={"tp": jnp.minimum(t + 1, n_tp - 1)}, device_id_type=MESH)

    def send_left(b, ch):
        return pltpu.make_async_remote_copy(
            sb.at[b, ch], rl.at[b, ch], send_sem.at[b, ch], rl_sem.at[b, ch],
            device_id={"tp": jnp.maximum(t - 1, 0)}, device_id_type=MESH)

    def place(i):
        q = lax.rem(i, per_phase)
        turn = q // nch
        c = lax.rem(q, nch)
        return turn, c, (i // per_phase) * nch + c

    def right_job(j, run):
        turn, _, ch = place(jnp.clip(j, 0, steps - 1))
        b = n_tp - 1 - turn

        @pl.when((j >= 0) & (j < steps) & (b > t))
        def _():
            run(b, ch)

    def left_job(j, run):
        turn, _, ch = place(jnp.clip(j, 0, steps - 1))

        @pl.when((j >= 0) & (j < steps) & (turn < t))
        def _():
            run(turn, ch)

    def wait_sends(i):
        right_job(i - t, lambda b, ch: send_right(b, ch).wait_send())
        left_job(i - (n_tp - 1 - t), lambda b, ch: send_left(b, ch).wait_send())

    def fill_angles():
        lane = lax.broadcasted_iota(jnp.int32, (1, HEAD), 1)
        half = HEAD // 2
        index = jnp.where(lane < half, lane, lane - half).astype(jnp.float32)
        frequency = jnp.exp(-jnp.log(jnp.float32(500000.0)) * 2.0 * index / HEAD)
        for j in range(pages):
            row = pos[j:j + 1, :].astype(jnp.float32)
            column = jnp.transpose(jnp.broadcast_to(row, (PAGE, PAGE)))
            angles = column * frequency
            sine = jnp.sin(angles)
            cos_s[j * PAGE:(j + 1) * PAGE, :] = jnp.cos(angles)
            sin_s[j * PAGE:(j + 1) * PAGE, :] = jnp.where(lane < half, -sine, sine)

    def own_sum(ch):
        acc[...] = jnp.dot(hb[t], wb[ch], preferred_element_type=jnp.float32)

        @pl.when(t > 0)
        def _():
            send_right(t, ch).wait_recv()
            acc[...] += rr[t, ch].astype(jnp.float32)

        @pl.when(t < n_tp - 1)
        def _():
            send_left(t, ch).wait_recv()
            acc[...] += rl[t, ch].astype(jnp.float32)

    def tp_copies(src, dst, send, recv, own):
        return [
            pltpu.make_async_remote_copy(
                src, dst.at[t if own else d], send.at[d], recv.at[d],
                device_id={"tp": lax.rem(t + d, n_tp)}, device_id_type=MESH)
            for d in range(1, n_tp)
        ]

    def peak_tp_copies():
        return tp_copies(peak_own, peak_tp, ptp_send, ptp_recv, False)

    def peak_seq_copies():
        return [
            pltpu.make_async_remote_copy(
                peak_mid, peak_seq.at[d], psq_send.at[d], psq_recv.at[d],
                device_id={"seq": lax.rem(s + d, n_seq)}, device_id_type=MESH)
            for d in range(1, n_seq)
        ]

    group = width // n_seq
    tile = bnd_seq.shape[2]

    def tile_of(other):
        return pl.ds(pl.multiple_of((other * group) // tile * tile, 128), tile)

    def bound_seq_copies():
        out = []
        for d in range(1, n_seq):
            other = lax.rem(s + d, n_seq)
            out.append(pltpu.make_async_remote_copy(
                bnd_own.at[:, tile_of(other)], bnd_seq.at[s], bsq_send.at[d], bsq_recv.at[d],
                device_id={"seq": other}, device_id_type=MESH))
        return out

    def bound_tp_copies():
        return tp_copies(bnd_seq, bnd_tp, btp_send, btp_recv, True)

    def key_sums():
        def one(c, carry):
            own_sum(c)
            total = acc[...]
            lanes = pl.ds(pl.multiple_of(c * CW, 128), CW)
            raw[:, lanes] = total
            peak_own[:, lanes] = jnp.max(jnp.abs(total).reshape(rows // 8, 8, CW), axis=0)
            return carry

        lax.fori_loop(0, nch, one, 0)
        for copy in peak_tp_copies():
            copy.start()

    def peak_middle():
        best = peak_own[...]
        for copy in peak_tp_copies():
            copy.wait_recv()
        for d in range(1, n_tp):
            best = jnp.maximum(best, peak_tp[d])
        peak_mid[...] = best
        for copy in peak_seq_copies():
            copy.start()

    def finish_keys():
        for copy in peak_seq_copies():
            copy.wait_recv()
        best = peak_mid[...]
        for d in range(1, n_seq):
            best = jnp.maximum(best, peak_seq[d])
        peak_tp[0] = best
        bnd_own[...] = jnp.zeros_like(bnd_own)

        def one(h, carry):
            lanes = pl.ds(pl.multiple_of(h * HEAD, 128), HEAD)
            peak = jnp.max(peak_tp[0, :, lanes], axis=0, keepdims=True)
            scale = (peak + 1e-06) / 7.0
            inverse = 1.0 / scale
            for j in range(pages):
                part = pl.ds(j * PAGE, PAGE)
                ratio = raw[part, lanes] * inverse
                code = (ratio - sine_of_turns(ratio) * (1.0 / (2.0 * math.pi))).astype(jnp.bfloat16)
                codes_s[part, lanes] = code
                dequant = code.astype(jnp.float32) * scale
                turned = dequant * cos_s[part, :] + pltpu.roll(dequant, HEAD // 2, 1) * sin_s[part, :]
                keys_s[part, lanes] = turned.astype(jnp.bfloat16)
                bnd_own[j:j + 1, lanes] = jnp.min(turned, axis=0, keepdims=True)
                bnd_own[pages + j:pages + j + 1, lanes] = jnp.max(turned, axis=0, keepdims=True)
            return carry

        lax.fori_loop(0, width // HEAD, one, 0)
        for copy in bound_seq_copies():
            copy.start()
        pltpu.make_async_copy(codes_s, codes_out, out_sem.at[0]).start()
        pltpu.make_async_copy(keys_s, keys_out, out_sem.at[1]).start()
        bnd_seq[s] = bnd_own[:, tile_of(s)]

    def bounds_middle():
        for copy in bound_seq_copies():
            copy.wait_recv()
        for copy in bound_tp_copies():
            copy.start()
        bnd_tp[t] = bnd_seq[...]

    def finish_bounds():
        for copy in bound_tp_copies():
            copy.wait_recv()
        channels = width // (n_seq * n_tp)
        inside = lax.rem(s * group, tile) + t * channels
        for side in range(2):
            bnd_pages[...] = jnp.zeros_like(bnd_pages)
            for a in range(n_seq):
                for b in range(n_tp):
                    first = (a * n_tp + b) * pages
                    bnd_pages[first:first + pages, :] = bnd_tp[b, a, side * pages:(side + 1) * pages, :]
            bnd_turned[...] = jnp.transpose(bnd_pages[...])
            mine = bnd_turned[pl.ds(pl.multiple_of(inside, 8), channels), :]
            bnd_res[side] = mine[:, :bnd_res.shape[2]]
        pltpu.make_async_copy(bnd_res, bounds_out, out_sem.at[2]).start()

    def forward_right(b, ch):
        @pl.when((t > 0) | (b < n_tp - 1) | (ch > 0))
        def _():
            acc[...] = jnp.dot(hb[b], wb[ch], preferred_element_type=jnp.float32)

            @pl.when(t > 0)
            def _():
                send_right(b, ch).wait_recv()
                acc[...] += rr[b, ch].astype(jnp.float32)

            sb[b, ch] = acc[...].astype(jnp.bfloat16)

        send_right(b, ch).start()

    def forward_left(b, ch):
        @pl.when((t < n_tp - 1) | (b > 0) | (ch > 0))
        def _():
            acc[...] = jnp.dot(hb[b], wb[ch], preferred_element_type=jnp.float32)

            @pl.when(t < n_tp - 1)
            def _():
                send_left(b, ch).wait_recv()
                acc[...] += rl[b, ch].astype(jnp.float32)

            sb[b, ch] = acc[...].astype(jnp.bfloat16)

        send_left(b, ch).start()

    def body(i, carry):
        turn, c, ch = place(jnp.minimum(i, steps - 1))

        @pl.when((turn == 0) & (i > 0) & (i < steps))
        def _():
            pltpu.make_async_copy(key_w.at[:, pl.ds(0, CW)], wb.at[ch], w_sem.at[ch]).wait()

        @pl.when(i == 1)
        def _():
            load_h(second).wait()

        for o in range(1, n_tp // 2):
            @pl.when(i == o * nch)
            def _(o=o):
                load_h(o).wait()
                load_h(n_tp - 1 - o).wait()

        wait_sends(i - DEPTH)
        right_job(i - t, forward_right)
        left_job(i - (n_tp - 1 - t), forward_left)

        for when, work in (
            (2, fill_angles),
            (per_phase, key_sums),
            (per_phase + 2, peak_middle),
            (per_phase + 5, finish_keys),
            (per_phase + 7, bounds_middle),
            (per_phase + 9, finish_bounds),
        ):
            pl.when(i == when)(work)
        return carry

    lax.fori_loop(0, steps + n_tp - 2, body, 0)

    def last(c, carry):
        own_sum(nch + c)
        values_s[c] = acc[...].astype(jnp.bfloat16)
        lanes = pl.ds(pl.multiple_of(c * CW, 128), CW)
        pltpu.make_async_copy(values_s.at[c], values_out.at[:, lanes], out_sem.at[3 + c]).start()
        return carry

    lax.fori_loop(0, nch, last, 0)

    def drain(i, carry):
        wait_sends(i)
        return carry

    lax.fori_loop(steps + n_tp - 2 - DEPTH, steps + n_tp - 2, drain, 0)
    for copy in peak_tp_copies() + peak_seq_copies() + bound_seq_copies() + bound_tp_copies():
        copy.wait_send()
    pltpu.make_async_copy(codes_s, codes_out, out_sem.at[0]).wait()
    pltpu.make_async_copy(keys_s, keys_out, out_sem.at[1]).wait()
    pltpu.make_async_copy(bnd_res, bounds_out, out_sem.at[2]).wait()
    for c in range(nch):
        pltpu.make_async_copy(values_s.at[c], values_out.at[:, pl.ds(c * CW, CW)], out_sem.at[3 + c]).wait()


def write_kernel(keys, values, codes, bounds, keys_out, values_out, codes_out, bounds_out, rows_s, bnd_in, bnd_s, in_sem, out_sem):
    parts = rows_s.shape[1]
    size = rows_s.shape[2]
    pairs = ((keys, keys_out), (values, values_out), (codes, codes_out))

    def fetch_rows(k, p):
        return pltpu.make_async_copy(pairs[k][0].at[pl.ds(p * size, size), :], rows_s.at[k, p], in_sem.at[k, p])

    def store_rows(k, p):
        return pltpu.make_async_copy(rows_s.at[k, p], pairs[k][1].at[pl.ds(p * size, size), :], out_sem.at[k, p])

    fetch = pltpu.make_async_copy(bounds, bnd_in, in_sem.at[3, 0])
    fetch.start()
    every = [(k, p) for p in range(parts) for k in range(3)]
    for k, p in every:
        fetch_rows(k, p).start()
    fetch.wait()
    for side in range(2):
        bnd_s[:, side, :] = bnd_in[side]
    store = pltpu.make_async_copy(bnd_s, bounds_out, out_sem.at[3, 0])
    store.start()
    for k, p in every:
        fetch_rows(k, p).wait()
        store_rows(k, p).start()
    for k, p in every:
        store_rows(k, p).wait()
    store.wait()


def write_out(keys, values, codes, bounds):
    rows, width = keys.shape
    parts = 3
    hbm = pl.BlockSpec(memory_space=pl.ANY)
    bound_shape = (bounds.shape[1], 2, bounds.shape[2])
    return pl.pallas_call(
        write_kernel,
        out_shape=[jax.ShapeDtypeStruct(a.shape, a.dtype) for a in (keys, values, codes)]
        + [jax.ShapeDtypeStruct(bound_shape, bounds.dtype)],
        in_specs=[hbm] * 4,
        out_specs=[hbm] * 4,
        scratch_shapes=[
            pltpu.VMEM((3, parts, rows // parts, width), keys.dtype),
            pltpu.VMEM(bounds.shape, bounds.dtype),
            pltpu.VMEM(bound_shape, bounds.dtype),
            pltpu.SemaphoreType.DMA((4, parts)),
            pltpu.SemaphoreType.DMA((4, parts)),
        ],
        compiler_params=pltpu.CompilerParams(vmem_limit_bytes=60 * 2**20),
        cost_estimate=pl.CostEstimate(flops=0, bytes_accessed=12 * rows * width, transcendentals=0),
    )(keys, values, codes, bounds)


def per_device(n_seq, n_tp, hidden_states, positions, key_weight, value_weight):
    depth, width = key_weight.shape
    rows = hidden_states.shape[0] // n_tp
    nch = width // CW
    pages = rows // PAGE
    all_pages = pages * n_seq * n_tp
    padded_pages = -(-all_pages // 128) * 128
    tile = max(128, width // n_seq)
    channels = width // (n_seq * n_tp)
    bf16, f32 = jnp.bfloat16, jnp.float32
    dma = pltpu.SemaphoreType.DMA
    hbm = pl.BlockSpec(memory_space=pl.ANY)
    keys, values, codes, bounds = pl.pallas_call(
        functools.partial(kernel, n_seq, n_tp),
        out_shape=(
            jax.ShapeDtypeStruct((rows, width), bf16),
            jax.ShapeDtypeStruct((rows, width), bf16),
            jax.ShapeDtypeStruct((rows, width), bf16),
            jax.ShapeDtypeStruct((2, channels, all_pages), f32),
        ),
        in_specs=[hbm, pl.BlockSpec(memory_space=pltpu.VMEM), hbm, hbm],
        out_specs=(hbm, hbm, hbm, hbm),
        scratch_shapes=[
            pltpu.VMEM((n_tp, rows, depth), bf16),
            pltpu.VMEM((2 * nch, depth, CW), bf16),
            pltpu.VMEM((n_tp, 2 * nch, rows, CW), bf16),
            pltpu.VMEM((n_tp, 2 * nch, rows, CW), bf16),
            pltpu.VMEM((n_tp, 2 * nch, rows, CW), bf16),
            pltpu.VMEM((rows, CW), f32),
            pltpu.VMEM((rows, width), f32),
            pltpu.VMEM((rows, HEAD), f32),
            pltpu.VMEM((rows, HEAD), f32),
            pltpu.VMEM((rows, width), bf16),
            pltpu.VMEM((rows, width), bf16),
            pltpu.VMEM((nch, rows, CW), bf16),
            pltpu.VMEM((8, width), f32),
            pltpu.VMEM((n_tp, 8, width), f32),
            pltpu.VMEM((8, width), f32),
            pltpu.VMEM((n_seq, 8, width), f32),
            pltpu.VMEM((8, width), f32),
            pltpu.VMEM((n_seq, 8, tile), f32),
            pltpu.VMEM((n_tp, n_seq, 8, tile), f32),
            pltpu.VMEM((padded_pages, tile), f32),
            pltpu.VMEM((tile, padded_pages), f32),
            pltpu.VMEM((2, channels, all_pages), f32),
            dma((n_tp,)),
            dma((2 * nch,)),
            dma((n_tp, 2 * nch)),
            dma((n_tp, 2 * nch)),
            dma((n_tp, 2 * nch)),
            dma((3 + nch,)),
            dma((n_tp,)), dma((n_tp,)),
            dma((n_seq,)), dma((n_seq,)),
            dma((n_seq,)), dma((n_seq,)),
            dma((n_tp,)), dma((n_tp,)),
        ],
        compiler_params=pltpu.CompilerParams(
            collective_id=0, has_side_effects=True, vmem_limit_bytes=56 * 2**20
        ),
        cost_estimate=pl.CostEstimate(
            flops=2 * n_tp * rows * depth * 2 * width,
            bytes_accessed=2 * (n_tp * rows * depth + 2 * depth * width + 3 * rows * width),
            transcendentals=0,
        ),
    )(hidden_states, positions.reshape(pages, PAGE), key_weight, value_weight)
    return write_out(keys, values, codes, bounds)


def solution(mesh):
    return jax.shard_map(
        functools.partial(per_device, mesh.shape["seq"], mesh.shape["tp"]),
        mesh=mesh,
        in_specs=(P("seq", "tp"), P(("seq", "tp")), P("tp", None), P("tp", None)),
        out_specs=(
            P(("seq", "tp"), None),
            P(("seq", "tp"), None),
            P(("seq", "tp"), None),
            P(("seq", "tp"), None, None),
        ),
        check_vma=False,
    )
```

```python
import functools
import math

import jax
import jax.numpy as jnp
from jax import lax
from jax.experimental import pallas as pl
from jax.experimental.pallas import tpu as pltpu
from jax.sharding import PartitionSpec as P

HEAD = 128
PAGE = 128
CW = 256
DEPTH = 12
MESH = pl.DeviceIdType.MESH


def sine_of_turns(turns):
    rest = turns - jnp.round(turns)
    size = jnp.abs(rest)
    x = (2.0 * math.pi) * jnp.minimum(size, 0.5 - size)
    y = x * x
    poly = jnp.float32(-1.0 / math.factorial(11))
    for order, sign in ((9, 1.0), (7, -1.0), (5, 1.0), (3, -1.0), (1, 1.0)):
        poly = poly * y + jnp.float32(sign / math.factorial(order))
    wave = poly * x
    return jnp.where(rest < 0.0, -wave, wave)


def kernel(
    n_seq, n_tp,
    hidden, pos_in, key_w, value_w,
    keys_out, values_out, codes_out, bounds_out,
    pos, hb, wb, sb, rr, rl, acc, raw, cos_s, sin_s,
    peak_own, peak_tp, peak_mid, peak_seq,
    bnd_own, bnd_seq, bnd_tp, bnd_pages, bnd_turned,
    pos_sem, h_sem, w_sem, send_sem, rr_sem, rl_sem,
    ptp_send, ptp_recv, psq_send, psq_recv, bsq_send, bsq_recv, btp_send, btp_recv,
):
    s = lax.axis_index("seq")
    t = lax.axis_index("tp")
    rows = hb.shape[1]
    width = raw.shape[1]
    nch = width // CW
    per_phase = (n_tp - 1) * nch
    steps = 2 * per_phase
    pages = rows // PAGE

    def load_h(b):
        return pltpu.make_async_copy(hidden.at[pl.ds(b * rows, rows), :], hb.at[b], h_sem.at[b])

    def load_w(ch):
        src = key_w if ch < nch else value_w
        return pltpu.make_async_copy(src.at[:, pl.ds((ch % nch) * CW, CW)], wb.at[ch], w_sem.at[ch])

    barrier = pltpu.get_barrier_semaphore()
    for d in range(1, n_tp):
        pl.semaphore_signal(barrier, inc=1, device_id={"tp": lax.rem(t + d, n_tp)}, device_id_type=MESH)
    for d in range(1, n_seq):
        pl.semaphore_signal(barrier, inc=1, device_id={"seq": lax.rem(s + d, n_seq)}, device_id_type=MESH)

    first = jnp.where(t < n_tp // 2, n_tp - 1, 0)
    second = n_tp - 1 - first
    piece, deep = rows // 3, wb.shape[1] // 2
    for k in range(2):
        part = pl.ds(k * deep, deep)
        pltpu.make_async_copy(key_w.at[part, pl.ds(0, CW)], wb.at[0, part], w_sem.at[0]).start()
    for k in range(3):
        pltpu.make_async_copy(
            hidden.at[pl.ds(first * rows + k * piece, piece), :], hb.at[first, pl.ds(k * piece, piece)], h_sem.at[first]
        ).start()

    load_w(0).wait()
    load_h(first).wait()
    for ch in range(1, nch):
        load_w(ch).start()
    load_h(second).start()
    load_pos = pltpu.make_async_copy(pos_in, pos, pos_sem.at[0])
    load_pos.start()
    for b in range(1, n_tp - 1):
        load_h(b).start()
    for ch in range(nch, 2 * nch):
        load_w(ch).start()

    @pl.when((t == 0) | (t == n_tp - 1))
    def _():
        sb[first, 0] = jnp.dot(hb[first], wb[0], preferred_element_type=jnp.float32).astype(jnp.bfloat16)

    pl.semaphore_wait(barrier, n_tp - 1 + n_seq - 1)

    def send_right(b, ch):
        return pltpu.make_async_remote_copy(
            sb.at[b, ch], rr.at[b, ch], send_sem.at[b, ch], rr_sem.at[b, ch],
            device_id={"tp": jnp.minimum(t + 1, n_tp - 1)}, device_id_type=MESH)

    def send_left(b, ch):
        return pltpu.make_async_remote_copy(
            sb.at[b, ch], rl.at[b, ch], send_sem.at[b, ch], rl_sem.at[b, ch],
            device_id={"tp": jnp.maximum(t - 1, 0)}, device_id_type=MESH)

    def place(i):
        q = lax.rem(i, per_phase)
        turn = q // nch
        c = lax.rem(q, nch)
        return turn, c, (i // per_phase) * nch + c

    def right_job(j, run):
        turn, _, ch = place(jnp.clip(j, 0, steps - 1))
        b = n_tp - 1 - turn

        @pl.when((j >= 0) & (j < steps) & (b > t))
        def _():
            run(b, ch)

    def left_job(j, run):
        turn, _, ch = place(jnp.clip(j, 0, steps - 1))

        @pl.when((j >= 0) & (j < steps) & (turn < t))
        def _():
            run(turn, ch)

    def wait_sends(i):
        right_job(i - t, lambda b, ch: send_right(b, ch).wait_send())
        left_job(i - (n_tp - 1 - t), lambda b, ch: send_left(b, ch).wait_send())

    def fill_angles():
        load_pos.wait()
        lane = lax.broadcasted_iota(jnp.int32, (1, HEAD), 1)
        half = HEAD // 2
        index = jnp.where(lane < half, lane, lane - half).astype(jnp.float32)
        frequency = jnp.exp(-jnp.log(jnp.float32(500000.0)) * 2.0 * index / HEAD)
        for j in range(pages):
            row = pos[j:j + 1, :].astype(jnp.float32)
            column = jnp.transpose(jnp.broadcast_to(row, (PAGE, PAGE)))
            angles = column * frequency
            sine = jnp.sin(angles)
            cos_s[j * PAGE:(j + 1) * PAGE, :] = jnp.cos(angles)
            sin_s[j * PAGE:(j + 1) * PAGE, :] = jnp.where(lane < half, -sine, sine)

    def own_sum(ch):
        acc[...] = jnp.dot(hb[t], wb[ch], preferred_element_type=jnp.float32)

        @pl.when(t > 0)
        def _():
            send_right(t, ch).wait_recv()
            acc[...] += rr[t, ch].astype(jnp.float32)

        @pl.when(t < n_tp - 1)
        def _():
            send_left(t, ch).wait_recv()
            acc[...] += rl[t, ch].astype(jnp.float32)

    def tp_copies(src, dst, send, recv, own):
        return [
            pltpu.make_async_remote_copy(
                src, dst.at[t if own else d], send.at[d], recv.at[d],
                device_id={"tp": lax.rem(t + d, n_tp)}, device_id_type=MESH)
            for d in range(1, n_tp)
        ]

    def peak_tp_copies():
        return tp_copies(peak_own, peak_tp, ptp_send, ptp_recv, False)

    def peak_seq_copies():
        return [
            pltpu.make_async_remote_copy(
                peak_mid, peak_seq.at[d], psq_send.at[d], psq_recv.at[d],
                device_id={"seq": lax.rem(s + d, n_seq)}, device_id_type=MESH)
            for d in range(1, n_seq)
        ]

    group = width // n_seq
    tile = bnd_seq.shape[2]

    def tile_of(other):
        return pl.ds(pl.multiple_of((other * group) // tile * tile, 128), tile)

    def bound_seq_copies():
        out = []
        for d in range(1, n_seq):
            other = lax.rem(s + d, n_seq)
            out.append(pltpu.make_async_remote_copy(
                bnd_own.at[:, tile_of(other)], bnd_seq.at[s], bsq_send.at[d], bsq_recv.at[d],
                device_id={"seq": other}, device_id_type=MESH))
        return out

    def bound_tp_copies():
        return tp_copies(bnd_seq, bnd_tp, btp_send, btp_recv, True)

    def key_sums():
        def one(c, carry):
            own_sum(c)
            total = acc[...]
            lanes = pl.ds(pl.multiple_of(c * CW, 128), CW)
            raw[:, lanes] = total
            peak_own[:, lanes] = jnp.max(jnp.abs(total).reshape(rows // 8, 8, CW), axis=0)
            return carry

        lax.fori_loop(0, nch, one, 0)
        for copy in peak_tp_copies():
            copy.start()

    def peak_middle():
        best = peak_own[...]
        for copy in peak_tp_copies():
            copy.wait_recv()
        for d in range(1, n_tp):
            best = jnp.maximum(best, peak_tp[d])
        peak_mid[...] = best
        for copy in peak_seq_copies():
            copy.start()

    def finish_keys():
        for copy in peak_seq_copies():
            copy.wait_recv()
        best = peak_mid[...]
        for d in range(1, n_seq):
            best = jnp.maximum(best, peak_seq[d])
        peak_tp[0] = best
        bnd_own[...] = jnp.zeros_like(bnd_own)

        def one(h, carry):
            lanes = pl.ds(pl.multiple_of(h * HEAD, 128), HEAD)
            peak = jnp.max(peak_tp[0, :, lanes], axis=0, keepdims=True)
            scale = (peak + 1e-06) / 7.0
            inverse = 1.0 / scale
            for j in range(pages):
                part = pl.ds(j * PAGE, PAGE)
                ratio = raw[part, lanes] * inverse
                code = (ratio - sine_of_turns(ratio) * (1.0 / (2.0 * math.pi))).astype(jnp.bfloat16)
                codes_out[part, lanes] = code
                dequant = code.astype(jnp.float32) * scale
                turned = dequant * cos_s[part, :] + pltpu.roll(dequant, HEAD // 2, 1) * sin_s[part, :]
                keys_out[part, lanes] = turned.astype(jnp.bfloat16)
                bnd_own[j:j + 1, lanes] = jnp.min(turned, axis=0, keepdims=True)
                bnd_own[pages + j:pages + j + 1, lanes] = jnp.max(turned, axis=0, keepdims=True)
            return carry

        lax.fori_loop(0, width // HEAD, one, 0)
        for copy in bound_seq_copies():
            copy.start()
        bnd_seq[s] = bnd_own[:, tile_of(s)]

    def bounds_middle():
        for copy in bound_seq_copies():
            copy.wait_recv()
        for copy in bound_tp_copies():
            copy.start()
        bnd_tp[t] = bnd_seq[...]

    def finish_bounds():
        for copy in bound_tp_copies():
            copy.wait_recv()
        channels = width // (n_seq * n_tp)
        inside = lax.rem(s * group, tile) + t * channels
        for side in range(2):
            bnd_pages[...] = jnp.zeros_like(bnd_pages)
            for a in range(n_seq):
                for b in range(n_tp):
                    first = (a * n_tp + b) * pages
                    bnd_pages[first:first + pages, :] = bnd_tp[b, a, side * pages:(side + 1) * pages, :]
            bnd_turned[...] = jnp.transpose(bnd_pages[...])
            mine = bnd_turned[pl.ds(pl.multiple_of(inside, 8), channels), :]
            bounds_out[side] = mine[:, :bounds_out.shape[2]]

    def forward_right(b, ch):
        @pl.when((t > 0) | (b < n_tp - 1) | (ch > 0))
        def _():
            acc[...] = jnp.dot(hb[b], wb[ch], preferred_element_type=jnp.float32)

            @pl.when(t > 0)
            def _():
                send_right(b, ch).wait_recv()
                acc[...] += rr[b, ch].astype(jnp.float32)

            sb[b, ch] = acc[...].astype(jnp.bfloat16)

        send_right(b, ch).start()

    def forward_left(b, ch):
        @pl.when((t < n_tp - 1) | (b > 0) | (ch > 0))
        def _():
            acc[...] = jnp.dot(hb[b], wb[ch], preferred_element_type=jnp.float32)

            @pl.when(t < n_tp - 1)
            def _():
                send_left(b, ch).wait_recv()
                acc[...] += rl[b, ch].astype(jnp.float32)

            sb[b, ch] = acc[...].astype(jnp.bfloat16)

        send_left(b, ch).start()

    def body(i, carry):
        turn, c, ch = place(jnp.minimum(i, steps - 1))

        @pl.when((turn == 0) & (i > 0) & (i < steps))
        def _():
            pltpu.make_async_copy(key_w.at[:, pl.ds(0, CW)], wb.at[ch], w_sem.at[ch]).wait()

        @pl.when(i == 1)
        def _():
            load_h(second).wait()

        for o in range(1, n_tp // 2):
            @pl.when(i == o * nch)
            def _(o=o):
                load_h(o).wait()
                load_h(n_tp - 1 - o).wait()

        wait_sends(i - DEPTH)
        right_job(i - t, forward_right)
        left_job(i - (n_tp - 1 - t), forward_left)

        for when, work in (
            (2, fill_angles),
            (per_phase, key_sums),
            (per_phase + 2, peak_middle),
            (per_phase + 5, finish_keys),
            (per_phase + 7, bounds_middle),
            (per_phase + 9, finish_bounds),
        ):
            pl.when(i == when)(work)
        return carry

    lax.fori_loop(0, steps + n_tp - 2, body, 0)

    def last(c, carry):
        own_sum(nch + c)
        values_out[:, pl.ds(pl.multiple_of(c * CW, 128), CW)] = acc[...].astype(jnp.bfloat16)
        return carry

    lax.fori_loop(0, nch, last, 0)

    def drain(i, carry):
        wait_sends(i)
        return carry

    lax.fori_loop(steps + n_tp - 2 - DEPTH, steps + n_tp - 2, drain, 0)
    for copy in peak_tp_copies() + peak_seq_copies() + bound_seq_copies() + bound_tp_copies():
        copy.wait_send()


def write_kernel(keys, values, codes, bounds, keys_out, values_out, codes_out, bounds_out, bnd_s, sem):
    half = keys.shape[0] // 2
    moves = []
    for k, (src, dst) in enumerate(((keys, keys_out), (values, values_out), (codes, codes_out))):
        for p in range(2):
            part = pl.ds(p * half, half)
            moves.append(pltpu.make_async_copy(src.at[part, :], dst.at[part, :], sem.at[2 * k + p]))
            moves[-1].start()
    for side in range(2):
        bnd_s[:, side, :] = bounds[side]
    moves.append(pltpu.make_async_copy(bnd_s, bounds_out, sem.at[6]))
    moves[-1].start()
    for move in moves:
        move.wait()


def write_out(keys, values, codes, bounds):
    hbm = pl.BlockSpec(memory_space=pl.ANY)
    bound_shape = (bounds.shape[1], 2, bounds.shape[2])
    return pl.pallas_call(
        write_kernel,
        out_shape=[jax.ShapeDtypeStruct(a.shape, a.dtype) for a in (keys, values, codes)]
        + [jax.ShapeDtypeStruct(bound_shape, bounds.dtype)],
        in_specs=[pl.BlockSpec(memory_space=pltpu.VMEM)] * 4,
        out_specs=[hbm] * 4,
        scratch_shapes=[pltpu.VMEM(bound_shape, bounds.dtype), pltpu.SemaphoreType.DMA((7,))],
        compiler_params=pltpu.CompilerParams(vmem_limit_bytes=8 * 2**20),
        cost_estimate=pl.CostEstimate(flops=0, bytes_accessed=12 * keys.size, transcendentals=0),
    )(keys, values, codes, bounds)


def per_device(n_seq, n_tp, hidden_states, positions, key_weight, value_weight):
    depth, width = key_weight.shape
    rows = hidden_states.shape[0] // n_tp
    nch = width // CW
    pages = rows // PAGE
    all_pages = pages * n_seq * n_tp
    padded_pages = -(-all_pages // 128) * 128
    tile = max(128, width // n_seq)
    channels = width // (n_seq * n_tp)
    bf16, f32 = jnp.bfloat16, jnp.float32
    dma = pltpu.SemaphoreType.DMA
    hbm = pl.BlockSpec(memory_space=pl.ANY)
    keys, values, codes, bounds = pl.pallas_call(
        functools.partial(kernel, n_seq, n_tp),
        out_shape=(
            jax.ShapeDtypeStruct((rows, width), bf16),
            jax.ShapeDtypeStruct((rows, width), bf16),
            jax.ShapeDtypeStruct((rows, width), bf16),
            jax.ShapeDtypeStruct((2, channels, all_pages), f32),
        ),
        in_specs=[pl.BlockSpec(memory_space=pltpu.HBM)] * 4,
        out_specs=(pl.BlockSpec(memory_space=pltpu.VMEM),) * 4,
        scratch_shapes=[
            pltpu.VMEM((pages, PAGE), jnp.int32),
            pltpu.VMEM((n_tp, rows, depth), bf16),
            pltpu.VMEM((2 * nch, depth, CW), bf16),
            pltpu.VMEM((n_tp, 2 * nch, rows, CW), bf16),
            pltpu.VMEM((n_tp, 2 * nch, rows, CW), bf16),
            pltpu.VMEM((n_tp, 2 * nch, rows, CW), bf16),
            pltpu.VMEM((rows, CW), f32),
            pltpu.VMEM((rows, width), f32),
            pltpu.VMEM((rows, HEAD), f32),
            pltpu.VMEM((rows, HEAD), f32),
            pltpu.VMEM((8, width), f32),
            pltpu.VMEM((n_tp, 8, width), f32),
            pltpu.VMEM((8, width), f32),
            pltpu.VMEM((n_seq, 8, width), f32),
            pltpu.VMEM((8, width), f32),
            pltpu.VMEM((n_seq, 8, tile), f32),
            pltpu.VMEM((n_tp, n_seq, 8, tile), f32),
            pltpu.VMEM((padded_pages, tile), f32),
            pltpu.VMEM((tile, padded_pages), f32),
            dma((1,)),
            dma((n_tp,)),
            dma((2 * nch,)),
            dma((n_tp, 2 * nch)),
            dma((n_tp, 2 * nch)),
            dma((n_tp, 2 * nch)),
            dma((n_tp,)), dma((n_tp,)),
            dma((n_seq,)), dma((n_seq,)),
            dma((n_seq,)), dma((n_seq,)),
            dma((n_tp,)), dma((n_tp,)),
        ],
        compiler_params=pltpu.CompilerParams(
            collective_id=0, has_side_effects=True, vmem_limit_bytes=48 * 2**20
        ),
        cost_estimate=pl.CostEstimate(
            flops=2 * n_tp * rows * depth * 2 * width,
            bytes_accessed=2 * (n_tp * rows * depth + 2 * depth * width + 3 * rows * width),
            transcendentals=0,
        ),
    )(hidden_states, positions.reshape(pages, PAGE), key_weight, value_weight)
    return write_out(keys, values, codes, bounds)


def solution(mesh):
    return jax.shard_map(
        functools.partial(per_device, mesh.shape["seq"], mesh.shape["tp"]),
        mesh=mesh,
        in_specs=(P("seq", "tp"), P(("seq", "tp")), P("tp", None), P("tp", None)),
        out_specs=(
            P(("seq", "tp"), None),
            P(("seq", "tp"), None),
            P(("seq", "tp"), None),
            P(("seq", "tp"), None, None),
        ),
        check_vma=False,
    )
```
